32 devices in a mesh: parts: 1, query: 16 (over z, y, x), blk: 2 (over core).
Axes of the slice: x: 2, y: 2, z: 4, core: 2. Of those that a mesh axis runs over, the one named last changes fastest.
Arguments:
- queries: bfloat16 [2, 256, 16384], P('blk', ('parts', 'query')), may hold values from -600 to 600, as said below
- cameras: bfloat16 [16, 512, 16384], P(('parts', 'query'), 'blk'), may hold values from -600 to 600, as said below
- query_block: int32 [16, 2, 16], P(('parts', 'query'), 'blk'), may hold values from 0 to 1
- camera_block: int32 [16, 2, 16], P(('parts', 'query'), 'blk'), may hold values from 0 to 3
- counts: int32 [16, 2], P(('parts', 'query'), 'blk'), may hold values from 1 to 16, as said below
Outputs:
- scores: float32 [16, 2, 16, 128, 128], P(('parts', 'query'), 'blk')
The draws below stay inside these ranges and needn't reach their ends.
Inputs may be any that keep to these rules, and one draw needn't show every extreme that they name: `queries`: finite values. `cameras`: finite values. `counts`: in every draw some list has all 16 slots live.
All inputs are finite; a program needn't handle non-finite values.
Results may differ from the reference program's by a relative error of at most 0.0003.
Values may be sent and summed in bfloat16 or wider, within the bound.
No kernel may reach another device: no remote copies, remote signals or barrier semaphores. Data moves between devices by JAX's collectives and lax.ppermute only.
A program may use at most 192 MiB of HBM per device.

```python
import math
import jax
import jax.numpy as jnp
from jax import lax

F = 16384
BLOCK = 128
KMAX = 16
QROWS = 256
QBLOCKS = 2
CROWS = 512
CBLOCKS = 4
N_QUERY = 16
N_BLK = 2


def scaled_rows(key, shape):
    key_base, key_row, key_col = jax.random.split(key, 3)
    row_shape = (shape[0], shape[1], 1)
    col_shape = (shape[0], 1, shape[2])
    base = jax.random.normal(key_base, shape, jnp.float32)
    upper = math.log(4.0)
    row_scale = jnp.exp(jax.random.uniform(key_row, row_shape, jnp.float32, 0.0, upper))
    col_scale = jnp.exp(jax.random.uniform(key_col, col_shape, jnp.float32, 0.0, upper))
    return jnp.clip(base * row_scale * col_scale, -600.0, 600.0)


def draw_queries(key, part):
    return scaled_rows(jax.random.fold_in(key, 11), (N_BLK, QROWS, F)).astype(jnp.bfloat16)


def draw_cameras(key, part):
    return scaled_rows(jax.random.fold_in(key, 23), (N_QUERY, CROWS, F)).astype(jnp.bfloat16)


def draw_counts(key, part):
    key_load, key_full = jax.random.split(jax.random.fold_in(key, 37))
    loads = jax.random.randint(key_load, (N_QUERY * N_BLK,), 1, KMAX + 1, dtype=jnp.int32)
    spot = jax.random.randint(key_full, (), 0, N_QUERY * N_BLK, dtype=jnp.int32)
    filled = jnp.where(jnp.arange(N_QUERY * N_BLK, dtype=jnp.int32) == spot, KMAX, loads)
    return filled.reshape(N_QUERY, N_BLK).astype(jnp.int32)


def place_ends(result, key, smallest, high):
    extent = result.shape
    spot = [jax.random.randint(jax.random.fold_in(key, axis), (), 0, extent[axis]) for axis in range(len(extent))]
    result = result.at[tuple(spot)].set(smallest)
    longest = extent.index(max(extent))
    spot[longest] = (spot[longest] + 1) % extent[longest]
    return result.at[tuple(spot)].set(high)


def setup_inputs(seed: int = 0, part: int = 0) -> dict:
    streams_of = jax.random.split(jax.random.key(seed), 6)
    own_keys = jax.random.split(jax.random.fold_in(streams_of[5], part), 6)
    queries = draw_queries(jax.random.fold_in(jax.random.fold_in(streams_of[5], part), 71), part)
    cameras = draw_cameras(jax.random.fold_in(jax.random.fold_in(streams_of[5], part), 71), part)
    query_block = place_ends(jax.random.randint(own_keys[2], (N_QUERY, N_BLK, KMAX), 0, QBLOCKS), jax.random.fold_in(own_keys[2], 1), 0, QBLOCKS - 1).astype(jnp.int32)
    camera_block = place_ends(jax.random.randint(own_keys[3], (N_QUERY, N_BLK, KMAX), 0, CBLOCKS), jax.random.fold_in(own_keys[3], 1), 0, CBLOCKS - 1).astype(jnp.int32)
    counts = draw_counts(jax.random.fold_in(jax.random.fold_in(streams_of[5], part), 71), part)
    return dict(queries=queries, cameras=cameras, query_block=query_block, camera_block=camera_block, counts=counts)


def inverse_rms(values):
    wide = values.astype(jnp.float32)
    return lax.rsqrt(lax.optimization_barrier(jnp.mean(wide * wide, axis=-1)) + 1e-06)

def reference(queries, cameras, query_block, camera_block, counts):
    query_scale = inverse_rms(queries)
    camera_scale = inverse_rms(cameras)
    inv_root = 1.0 / math.sqrt(F)
    entries = jnp.arange(N_QUERY * N_BLK * KMAX, dtype=jnp.int32)

    def score_entry(entry_index):
        group_index = entry_index // (N_BLK * KMAX)
        set_index = entry_index // KMAX % N_BLK
        slot_index = entry_index % KMAX
        query_start = (query_block[group_index, set_index, slot_index] * BLOCK).astype(jnp.int32)
        camera_start = (camera_block[group_index, set_index, slot_index] * BLOCK).astype(jnp.int32)
        zero_index = jnp.zeros((), jnp.int32)
        query_rows = lax.dynamic_slice(queries, (set_index, query_start, zero_index), (1, BLOCK, F))[0]
        camera_rows = lax.dynamic_slice(cameras, (group_index, camera_start, zero_index), (1, BLOCK, F))[0]
        products = lax.dot_general(query_rows, camera_rows, (((1,), (1,)), ((), ())), preferred_element_type=jnp.float32)
        query_norms = lax.dynamic_slice(query_scale, (set_index, query_start), (1, BLOCK))[0]
        camera_norms = lax.dynamic_slice(camera_scale, (group_index, camera_start), (1, BLOCK))[0]
        scored = products * query_norms[:, None] * camera_norms[None, :] * inv_root
        return jnp.where(slot_index < counts[group_index, set_index], scored, jnp.zeros_like(scored))
    scores = lax.map(score_entry, entries)
    return scores.reshape(N_QUERY, N_BLK, KMAX, BLOCK, BLOCK)
```

```python
import functools
import math

import jax
import jax.numpy as jnp
from jax import lax
from jax.experimental import pallas as pl
from jax.experimental.pallas import tpu as pltpu
from jax.sharding import PartitionSpec as P

BLOCK = 128
CHUNK = 2048


def inverse_rms(values):
    wide = values.astype(jnp.float32)
    return lax.rsqrt(jnp.mean(wide * wide, axis=-1) + 1e-06)


def gathered_units(own, axis):
    devices = lax.axis_size(axis)
    rings = devices // 4
    half = own.shape[1] // 2
    me = lax.axis_index(axis)

    def swapped(x, bit):
        return lax.ppermute(x, axis, [(i, i ^ bit) for i in range(devices)])

    def turned(x, by):
        return lax.ppermute(x, axis, [(i, (i + 4 * by) % devices) for i in range(devices)])

    def first(x):
        return x[:, :half]

    def second(x):
        return x[:, half:]

    own_halves = (first(own), second(own))
    y_first = swapped(own_halves[0], 2)
    x_second = swapped(own_halves[1], 1)
    column = {0: own}
    column[1] = turned(own, 1)
    x_first = swapped(own_halves[0], 1)
    y_second = swapped(own_halves[1], 2)
    column[rings - 1] = turned(own, -1)
    for k in range(2, rings // 2 + 1):
        column[k] = turned(column[k - 1], 1)
    for k in range(rings - 2, rings // 2, -1):
        column[k] = turned(column[k + 1], -1)
    across_x = {0: (x_first, x_second)}
    across_y = {0: (y_first, y_second)}
    diagonal = {0: (swapped(y_first, 1), swapped(x_second, 2))}
    for k in range(1, rings):
        across_x[k] = (swapped(column[k], 1),)
        across_y[k] = (swapped(column[k], 2),)
    diagonal[1] = (swapped(first(across_y[1][0]), 1), swapped(second(across_x[1][0]), 2))
    for k in range(rings - 1, rings // 2, -1):
        diagonal[k] = tuple(turned(part, -1) for part in diagonal[(k + 1) % rings])
    for k in range(2, rings // 2 + 1):
        diagonal[k] = tuple(turned(part, 1) for part in diagonal[k - 1])

    units = []
    for k in range(rings):
        source = (me - 4 * k) % devices
        units.append(((column[k],), source))
        units.append((across_x[k], source ^ 1))
        units.append((across_y[k], source ^ 2))
        units.append((diagonal[k], source ^ 3))
    return units


def score_kernel(layout, steps, slots, *refs):
    sources, query_block, camera_block, counts, query_scale, camera_scale = refs[:6]
    pieces = refs[6 : 6 + sum(layout)]
    near, far, out, total, placed = refs[6 + sum(layout) :]
    step = pl.program_id(0)
    rows = pieces[0].shape[0]
    tile = near.shape[0]

    @pl.when(step == 0)
    def _():
        total[...] = jnp.zeros_like(total)

    def add(part):
        chosen, at = [], 0
        for count in layout:
            chosen.append(pieces[at + (part if count == 2 else 0)][...])
            at += count
        panel = jnp.concatenate(chosen, axis=0)
        for at, cameras in enumerate((near, far)):
            total[:, at * tile : (at + 1) * tile] += lax.dot_general(
                panel, cameras[...], (((1,), (1,)), ((), ())), preferred_element_type=jnp.float32
            )

    @pl.when(step < steps // 2)
    def _():
        add(0)

    @pl.when(step >= steps // 2)
    def _():
        add(1)

    @pl.when(step == steps - 1)
    def _():
        for unit in range(len(layout)):
            start = pl.multiple_of(sources[unit] * rows, rows)
            scaled = total[unit * rows : (unit + 1) * rows, :] * camera_scale[...]
            placed[pl.ds(start, rows), :] = scaled * query_scale[pl.ds(start, rows), :]
        for slot in range(slots):
            @pl.when(slot < counts[0, 0])
            def _():
                row = pl.multiple_of(query_block[0, 0, slot] * BLOCK, BLOCK)
                column = pl.multiple_of(camera_block[0, 0, slot] * BLOCK, BLOCK)
                out[slot] = placed[pl.ds(row, BLOCK), pl.ds(column, BLOCK)]

            @pl.when(slot >= counts[0, 0])
            def _():
                out[slot] = jnp.zeros((BLOCK, BLOCK), jnp.float32)


def shards(queries, cameras, query_block, camera_block, counts):
    own = queries[0]
    mine = cameras[0]
    rows, features = own.shape
    tile = mine.shape[0]
    cores = lax.axis_size("blk")
    core = lax.axis_index("blk")
    slots = query_block.shape[2]
    query_scale = lax.all_gather(inverse_rms(own), "query", axis=0, tiled=True)
    other = lax.ppermute(mine, "blk", [(i, (i + 1) % cores) for i in range(cores)])
    units = gathered_units(own, "query")

    scale_near, scale_far = inverse_rms(mine), inverse_rms(other)
    camera_scale = jnp.concatenate([scale_near, scale_far])[None] * (1.0 / math.sqrt(features))
    block_places = tile // BLOCK
    owner = camera_block // block_places
    place = (core - owner) % cores * block_places + camera_block % block_places

    steps = features // CHUNK
    layout = tuple(len(parts) for parts, _ in units)
    sources = jnp.stack([source for _, source in units]).astype(jnp.int32)
    pieces = [piece for parts, _ in units for piece in parts]
    piece_specs = []
    for count in layout:
        if count == 1:
            piece_specs.append(pl.BlockSpec((rows, CHUNK), lambda i: (0, i)))
        else:
            piece_specs.append(pl.BlockSpec((rows, CHUNK), lambda i: (0, jnp.minimum(i, steps // 2 - 1))))
            piece_specs.append(pl.BlockSpec((rows, CHUNK), lambda i: (0, jnp.maximum(i - steps // 2, 0))))
    scalars = pl.BlockSpec(memory_space=pltpu.SMEM)
    whole = lambda *shape: pl.BlockSpec(shape, lambda i: (0,) * len(shape))
    query_rows = rows * len(units)
    camera_rows = tile * cores
    scores = pl.pallas_call(
        functools.partial(score_kernel, layout, steps, slots),
        grid=(steps,),
        in_specs=[scalars] * 4
        + [whole(query_rows, 1), whole(1, camera_rows)]
        + piece_specs
        + [pl.BlockSpec((tile, CHUNK), lambda i: (0, i))] * 2,
        out_specs=whole(slots, BLOCK, BLOCK),
        out_shape=jax.ShapeDtypeStruct((slots, BLOCK, BLOCK), jnp.float32),
        scratch_shapes=[
            pltpu.VMEM((query_rows, camera_rows), jnp.float32),
            pltpu.VMEM((query_rows, camera_rows), jnp.float32),
        ],
        compiler_params=pltpu.CompilerParams(vmem_limit_bytes=24 * 1024 * 1024),
        cost_estimate=pl.CostEstimate(
            flops=2 * query_rows * camera_rows * features,
            bytes_accessed=2 * features * (query_rows + camera_rows),
            transcendentals=0,
        ),
        name="scores",
    )(sources, query_block, place, counts, query_scale[:, None], camera_scale, *pieces, mine, other)
    return scores[None, None]


def solution(mesh):
    placed = (
        P("blk", ("parts", "query"), None),
        P(("parts", "query"), "blk", None),
        P(("parts", "query"), "blk", None),
        P(("parts", "query"), "blk", None),
        P(("parts", "query"), "blk"),
    )
    return jax.shard_map(
        shards,
        mesh=mesh,
        in_specs=placed,
        out_specs=P(("parts", "query"), "blk", None, None, None),
        check_vma=False,
    )
```

```python
import functools
import math

import jax
import jax.numpy as jnp
from jax import lax
from jax.experimental import pallas as pl
from jax.experimental.pallas import tpu as pltpu
from jax.sharding import PartitionSpec as P

BLOCK = 128
CHUNK = 4096


def inverse_rms(values):
    wide = values.astype(jnp.float32)
    return lax.rsqrt(jnp.mean(wide * wide, axis=-1) + 1e-06)


def gathered_units(own, axis):
    devices = lax.axis_size(axis)
    rings = devices // 4
    half = own.shape[1] // 2
    me = lax.axis_index(axis)

    def swapped(x, bit):
        return lax.ppermute(x, axis, [(i, i ^ bit) for i in range(devices)])

    def turned(x, by):
        return lax.ppermute(x, axis, [(i, (i + 4 * by) % devices) for i in range(devices)])

    def first(x):
        return x[:, :half]

    def second(x):
        return x[:, half:]

    own_halves = (first(own), second(own))
    y_first = swapped(own_halves[0], 2)
    x_second = swapped(own_halves[1], 1)
    column = {0: own}
    column[1] = turned(own, 1)
    x_first = swapped(own_halves[0], 1)
    y_second = swapped(own_halves[1], 2)
    column[rings - 1] = turned(own, -1)
    for k in range(2, rings // 2 + 1):
        column[k] = turned(column[k - 1], 1)
    for k in range(rings - 2, rings // 2, -1):
        column[k] = turned(column[k + 1], -1)
    across_x = {0: (x_first, x_second)}
    across_y = {0: (y_first, y_second)}
    diagonal = {0: (swapped(y_first, 1), swapped(x_second, 2))}
    for k in range(1, rings):
        across_x[k] = (swapped(column[k], 1),)
        across_y[k] = (swapped(column[k], 2),)
    diagonal[1] = (swapped(first(across_y[1][0]), 1), swapped(second(across_x[1][0]), 2))
    for k in range(rings - 1, rings // 2, -1):
        diagonal[k] = tuple(turned(part, -1) for part in diagonal[(k + 1) % rings])
    for k in range(2, rings // 2 + 1):
        diagonal[k] = tuple(turned(part, 1) for part in diagonal[k - 1])

    def source(k, flip):
        return (me - 4 * k) % devices ^ flip

    middle = rings // 2
    groups = [[] for _ in range(rings)]
    for k in range(rings):
        group = 0 if k == 0 else rings - 1 if k == middle else 1 + (k if k < middle else k - 1) // 4
        groups[group].append(((column[k],), source(k, 0)))
        groups[group].append((across_x[k], source(k, 1)))
        groups[group].append((across_y[k], source(k, 2)))
        groups[0 if k == 0 else rings - 1].append((diagonal[k], source(k, 3)))
    return [group for group in groups if group]


def add_products(layout, pieces, near, far, total, scale):
    features = near.shape[1]
    half = features // 2
    chunk = min(CHUNK, half)
    total[...] = jnp.zeros_like(total)
    scale[...] = jnp.zeros_like(scale)
    tile = near.shape[0]
    for part in range(2):

        @pl.loop(0, half // chunk)
        def _(step):
            inside = pl.multiple_of(step * chunk, chunk)
            along = pl.ds(part * half + inside, chunk)
            chosen, at = [], 0
            for count in layout:
                if count == 1:
                    chosen.append(pieces[at][:, along])
                else:
                    chosen.append(pieces[at + part][:, pl.ds(inside, chunk)])
                at += count
            panel = jnp.concatenate(chosen, axis=0)
            for at, cameras in enumerate((near, far)):
                total[at * tile : (at + 1) * tile, :] += lax.dot_general(
                    cameras[:, along], panel, (((1,), (1,)), ((), ())), preferred_element_type=jnp.float32
                )
            wide = panel.astype(jnp.float32)
            scale[...] += jnp.sum(wide * wide, axis=-1, keepdims=True)

    scale[...] = lax.rsqrt(scale[...] * (1.0 / features) + 1e-06)


def part_kernel(layout, *refs):
    pieces = refs[: sum(layout)]
    near, far, products, total, scale = refs[sum(layout) :]
    add_products(layout, pieces, near, far, total, scale)
    products[...] = total[...].T * scale[...]


def last_kernel(layout, parts, slots, *refs):
    sources, query_block, camera_block, counts, camera_scale = refs[:5]
    earlier = refs[5 : 5 + parts]
    pieces = refs[5 + parts : 5 + parts + sum(layout)]
    near, far, out, total, scale, placed = refs[5 + parts + sum(layout) :]
    rows = pieces[0].shape[0]
    add_products(layout, pieces, near, far, total, scale)
    products = total[...].T * scale[...]
    unit = 0
    for part in earlier:
        for at in range(part.shape[0] // rows):
            start = pl.multiple_of(sources[unit] * rows, rows)
            placed[pl.ds(start, rows), :] = part[at * rows : (at + 1) * rows, :] * camera_scale[...]
            unit += 1
    for at in range(len(layout)):
        start = pl.multiple_of(sources[unit] * rows, rows)
        placed[pl.ds(start, rows), :] = products[at * rows : (at + 1) * rows, :] * camera_scale[...]
        unit += 1
    for slot in range(slots):

        @pl.when(slot < counts[0, 0])
        def _():
            row = pl.multiple_of(query_block[0, 0, slot] * BLOCK, BLOCK)
            column = pl.multiple_of(camera_block[0, 0, slot] * BLOCK, BLOCK)
            out[slot] = placed[pl.ds(row, BLOCK), pl.ds(column, BLOCK)]

        @pl.when(slot >= counts[0, 0])
        def _():
            out[slot] = jnp.zeros((BLOCK, BLOCK), jnp.float32)


def shards(queries, cameras, query_block, camera_block, counts):
    own = queries[0]
    mine = cameras[0]
    rows, features = own.shape
    tile = mine.shape[0]
    cores = lax.axis_size("blk")
    core = lax.axis_index("blk")
    slots = query_block.shape[2]
    other = lax.ppermute(mine, "blk", [(i, (i + 1) % cores) for i in range(cores)])
    groups = gathered_units(own, "query")

    scale_near, scale_far = inverse_rms(mine), inverse_rms(other)
    camera_scale = jnp.concatenate([scale_near, scale_far])[None] * (1.0 / math.sqrt(features))
    block_places = tile // BLOCK
    owner = camera_block // block_places
    place = (core - owner) % cores * block_places + camera_block % block_places
    sources = jnp.stack([source for group in groups for _, source in group]).astype(jnp.int32)
    camera_rows = tile * cores
    vmem = pl.BlockSpec(memory_space=pltpu.VMEM)
    smem = pl.BlockSpec(memory_space=pltpu.SMEM)

    def call(kernel, group, operands, specs, shape, more, name):
        layout = tuple(len(parts) for parts, _ in group)
        pieces = [piece for parts, _ in group for piece in parts]
        count = rows * len(group)
        return pl.pallas_call(
            functools.partial(kernel, layout),
            in_specs=specs + [vmem] * (len(pieces) + 2),
            out_specs=vmem,
            out_shape=jax.ShapeDtypeStruct(shape, jnp.float32),
            scratch_shapes=[
                pltpu.VMEM((camera_rows, count), jnp.float32),
                pltpu.VMEM((count, 1), jnp.float32),
            ]
            + more,
            compiler_params=pltpu.CompilerParams(vmem_limit_bytes=40 * 1024 * 1024),
            cost_estimate=pl.CostEstimate(
                flops=2 * count * camera_rows * features,
                bytes_accessed=2 * features * (count + camera_rows),
                transcendentals=0,
            ),
            name=name,
        )(*operands, *pieces, mine, other)

    earlier = [
        call(part_kernel, group, [], [], (rows * len(group), camera_rows), [], "products")
        for group in groups[:-1]
    ]
    query_rows = rows * sum(len(group) for group in groups)

    def closing(layout, *refs):
        last_kernel(layout, len(earlier), slots, *refs)

    scores = call(
        closing,
        groups[-1],
        [sources, query_block, place, counts, camera_scale] + earlier,
        [smem] * 4 + [vmem] * (1 + len(earlier)),
        (slots, BLOCK, BLOCK),
        [pltpu.VMEM((query_rows, camera_rows), jnp.float32)],
        "scores",
    )
    return scores[None, None]


def solution(mesh):
    placed = (
        P("blk", ("parts", "query"), None),
        P(("parts", "query"), "blk", None),
        P(("parts", "query"), "blk", None),
        P(("parts", "query"), "blk", None),
        P(("parts", "query"), "blk"),
    )
    return jax.shard_map(
        shards,
        mesh=mesh,
        in_specs=placed,
        out_specs=P(("parts", "query"), "blk", None, None, None),
        check_vma=False,
    )
```

```python
import functools
import math

import jax
import jax.numpy as jnp
from jax import lax
from jax.experimental import pallas as pl
from jax.experimental.pallas import tpu as pltpu
from jax.sharding import PartitionSpec as P

BLOCK = 128
CHUNK = 4096
VMEM_LIMIT = 48 * 1024 * 1024
LATE = 5


def exchanged(own, mine, axis, core_axis):
    devices = lax.axis_size(axis)
    cores = lax.axis_size(core_axis)
    rings = devices // 4

    def swap(bit):
        return [(i, i ^ bit) for i in range(devices)]

    def turn(by):
        return [(i, (i + 4 * by) % devices) for i in range(devices)]

    outward = []
    for k in range(1, rings // 2 + 1):
        outward += [k] if k == rings - k else [k, rings - k]

    def column(k):
        back = k > rings // 2
        return (0, k), (0, (k + 1) % rings if back else k - 1), turn(-1 if back else 1)

    def across(bit, k):
        return (bit, k), (0, k), swap(bit)

    def diagonal(k):
        if k < 2:
            return (3, k), ((1, k), (2, k))[k], swap((2, 1)[k])
        return (3, k), (3, (k + 1) % rings), turn(-1)

    other = "other"
    ops = [(column(outward[0]), None), (across(1, 0), None), (across(2, 0), None), (other, None)]
    ops += [(across(1, outward[0]), None), (diagonal(0), None)]
    ops += [(column(k), other) for k in outward[1:2]]
    ops += [(across(2, outward[0]), (2, 0))]
    for at, k in enumerate(outward[1:], 1):
        ops += [(column(later), (1, outward[at - 1])) for later in outward[at + 1 : at + 2]]
        ops += [(across(1, k), None), (across(2, k), (3, 0) if at == 1 else None)]
        ops += [(diagonal(rings - at), None)] + [(diagonal(1), None)] * (at == 1)

    pieces = {(0, 0): own}
    landed = [(0, 0)]
    for op, gate in ops:
        if op is other:
            key, operand, over, pairs = other, mine, core_axis, [(i, (i + 1) % cores) for i in range(cores)]
        else:
            key, source, pairs = op
            operand, over = pieces[source], axis
            if gate is not None:
                operand, pieces[gate] = lax.optimization_barrier((operand, pieces[gate]))
        pieces[key] = lax.ppermute(operand, over, pairs)
        if op is not other:
            landed.append(key)
    return pieces.pop(other), {key: pieces[key] for key in landed}


def add_products(pieces, near, far, total, squares, camera_squares=None):
    tile = near.shape[0]
    panel = jnp.concatenate([piece[...] for piece in pieces], axis=0)
    for at, cameras in enumerate((near, far)):
        block = cameras[...]
        total[at * tile : (at + 1) * tile, :] += lax.dot_general(
            block, panel, (((1,), (1,)), ((), ())), preferred_element_type=jnp.float32
        )
        if camera_squares is not None:
            wide = block.astype(jnp.float32)
            camera_squares[at * tile : (at + 1) * tile, :] += jnp.sum(wide * wide, axis=-1, keepdims=True)
    wide = panel.astype(jnp.float32)
    squares[...] += jnp.sum(wide * wide, axis=-1, keepdims=True)


def inverse_rms(squares, features):
    return lax.rsqrt(squares * (1.0 / features) + 1e-06)


def first_kernel(features, count, *refs):
    pieces = refs[:count]
    near, far, products, camera_scale, total, squares = refs[count:]

    @pl.when(pl.program_id(0) == 0)
    def _():
        total[...] = jnp.zeros_like(total)
        squares[...] = jnp.zeros_like(squares)
        camera_scale[...] = jnp.zeros_like(camera_scale)

    add_products(pieces, near, far, total, squares, camera_scale)

    @pl.when(pl.program_id(0) == pl.num_programs(0) - 1)
    def _():
        camera_scale[...] = inverse_rms(camera_scale[...], features) * (1.0 / math.sqrt(features))
        products[...] = (total[...] * camera_scale[...]).T * inverse_rms(squares[...], features)


def last_kernel(features, count, *refs):
    sources, query_block, camera_block, counts, camera_scale, earlier = refs[:6]
    pieces = refs[6 : 6 + count]
    near, far, out, total, squares, placed = refs[6 + count :]
    rows = pieces[0].shape[0]
    early = earlier.shape[0] // rows

    @pl.when(pl.program_id(0) == 0)
    def _():
        total[...] = jnp.zeros_like(total)
        squares[...] = jnp.zeros_like(squares)
        for unit in range(early):
            start = pl.multiple_of(sources[unit] * rows, rows)
            placed[pl.ds(start, rows), :] = earlier[unit * rows : (unit + 1) * rows, :]

    add_products(pieces, near, far, total, squares)

    @pl.when(pl.program_id(0) == pl.num_programs(0) - 1)
    def _():
        products = (total[...] * camera_scale[...]).T * inverse_rms(squares[...], features)
        for unit in range(count):
            start = pl.multiple_of(sources[early + unit] * rows, rows)
            placed[pl.ds(start, rows), :] = products[unit * rows : (unit + 1) * rows, :]
        for slot in range(out.shape[0]):

            @pl.when(slot < counts[0, 0])
            def _():
                row = pl.multiple_of(query_block[0, 0, slot] * BLOCK, BLOCK)
                column = pl.multiple_of(camera_block[0, 0, slot] * BLOCK, BLOCK)
                out[slot] = placed[pl.ds(row, BLOCK), pl.ds(column, BLOCK)]

            @pl.when(slot >= counts[0, 0])
            def _():
                out[slot] = jnp.zeros((BLOCK, BLOCK), jnp.float32)


def shards(queries, cameras, query_block, camera_block, counts):
    own = queries[0]
    mine = cameras[0]
    rows, features = own.shape
    tile = mine.shape[0]
    cores = lax.axis_size("blk")
    core = lax.axis_index("blk")
    devices = lax.axis_size("query")
    me = lax.axis_index("query")
    slots = query_block.shape[2]
    other, units = exchanged(own, mine, "query", "blk")

    block_places = tile // BLOCK
    owner = camera_block // block_places
    place = (core - owner) % cores * block_places + camera_block % block_places
    camera_rows = tile * cores
    sources = jnp.stack([(me - 4 * k) % devices ^ flip for flip, k in units]).astype(jnp.int32)
    smem = pl.BlockSpec(memory_space=pltpu.SMEM)

    def whole(*shape):
        return pl.BlockSpec(shape, lambda step: (0,) * len(shape))

    def chunk(height):
        return pl.BlockSpec((height, CHUNK), lambda step: (0, step))

    def call(kernel, chosen, operands, specs, shapes, more, name):
        count = rows * len(chosen)
        return pl.pallas_call(
            functools.partial(kernel, features, len(chosen)),
            grid=(features // CHUNK,),
            in_specs=specs + [chunk(rows)] * len(chosen) + [chunk(tile)] * 2,
            out_specs=[whole(*shape) for shape in shapes],
            out_shape=[jax.ShapeDtypeStruct(shape, jnp.float32) for shape in shapes],
            scratch_shapes=[
                pltpu.VMEM((camera_rows, count), jnp.float32),
                pltpu.VMEM((count, 1), jnp.float32),
            ]
            + more,
            compiler_params=pltpu.CompilerParams(vmem_limit_bytes=VMEM_LIMIT),
            cost_estimate=pl.CostEstimate(
                flops=2 * count * camera_rows * features,
                bytes_accessed=2 * features * (count + camera_rows),
                transcendentals=0,
            ),
            name=name,
        )(*operands, *chosen, mine, other)

    arrived = list(units.values())
    early, late = arrived[:-LATE], arrived[-LATE:]
    products, camera_scale = call(
        first_kernel, early, [], [], [(rows * len(early), camera_rows), (camera_rows, 1)], [], "products"
    )
    (scores,) = call(
        last_kernel,
        late,
        [sources, query_block, place, counts, camera_scale, products],
        [smem] * 4 + [whole(*camera_scale.shape), whole(*products.shape)],
        [(slots, BLOCK, BLOCK)],
        [pltpu.VMEM((rows * len(arrived), camera_rows), jnp.float32)],
        "scores",
    )
    return scores[None, None]


def solution(mesh):
    placed = (
        P("blk", ("parts", "query"), None),
        P(("parts", "query"), "blk", None),
        P(("parts", "query"), "blk", None),
        P(("parts", "query"), "blk", None),
        P(("parts", "query"), "blk"),
    )
    return jax.shard_map(
        shards,
        mesh=mesh,
        in_specs=placed,
        out_specs=P(("parts", "query"), "blk", None, None, None),
        check_vma=False,
    )
```

```python
import math

import jax
import jax.numpy as jnp
from jax import lax
from jax.experimental import pallas as pl
from jax.experimental.pallas import tpu as pltpu
from jax.sharding import PartitionSpec as P

BLOCK = 128
CHUNK = 4096
AHEAD = 2
LATE = 3
VMEM_LIMIT = 20 * 1024 * 1024


def add_products(panel, cameras, total, squares):
    at = 0
    for tile in cameras:
        total[at : at + tile.shape[0], :] += lax.dot_general(
            tile, panel, (((1,), (1,)), ((), ())), preferred_element_type=jnp.float32
        )
        at += tile.shape[0]
    wide = panel.astype(jnp.float32)
    squares[...] += jnp.sum(wide * wide, axis=-1, keepdims=True)


def inverse_rms(squares, features):
    return lax.rsqrt(squares * (1.0 / features) + 1e-06)


def chunks_of(sources, targets, sems):
    steps = sources[0].shape[1] // CHUNK
    steps_held = [target.shape[1] // CHUNK for target in targets]

    def at(step, count):
        return pl.ds(step % count * CHUNK, CHUNK)

    def copies(step):
        return [
            pltpu.make_async_copy(
                source.at[:, at(step, steps)], target.at[:, at(step, count)], sems.at[index, step % steps]
            )
            for index, (source, target, count) in enumerate(zip(sources, targets, steps_held))
        ]

    return steps, copies, lambda step: [target[:, at(step, count)] for target, count in zip(targets, steps_held)]


def early_kernel(pieces, own, mine, other, products, camera_scale, total, squares, held, near, far, sems):
    features = own.shape[1]
    steps, copies, chunks = chunks_of((mine, other, own), (near, far, held), sems)
    for step in range(min(AHEAD, steps)):
        for copy in copies(step):
            copy.start()
    total[...] = jnp.zeros_like(total)
    squares[...] = jnp.zeros_like(squares)
    camera_scale[...] = jnp.zeros_like(camera_scale)
    for step in range(steps):
        for copy in copies(step):
            copy.wait()
        *cameras, rows = chunks(step)
        along = pl.ds(step * CHUNK, CHUNK)
        add_products(jnp.concatenate([rows] + [piece[:, along] for piece in pieces], axis=0), cameras, total, squares)
        at = 0
        for tile in cameras:
            wide = tile.astype(jnp.float32)
            camera_scale[at : at + tile.shape[0], :] += jnp.sum(wide * wide, axis=-1, keepdims=True)
            at += tile.shape[0]
        if step + AHEAD < steps:
            for copy in copies(step + AHEAD):
                copy.start()
    camera_scale[...] = inverse_rms(camera_scale[...], features) * (1.0 / math.sqrt(features))
    products[...] = (total[...] * camera_scale[...]).T * inverse_rms(squares[...], features)


def middle_kernel(pieces, mine, other, camera_scale, products, near, far, total, squares, sems):
    features = near.shape[1]
    steps, copies, chunks = chunks_of((mine, other), (near, far), sems)
    for step in range(min(AHEAD, steps)):
        for copy in copies(step):
            copy.start()
    total[...] = jnp.zeros_like(total)
    squares[...] = jnp.zeros_like(squares)
    for step in range(steps):
        for copy in copies(step):
            copy.wait()
        if step + AHEAD < steps:
            for copy in copies(step + AHEAD):
                copy.start()
        along = pl.ds(step * CHUNK, CHUNK)
        add_products(jnp.concatenate([piece[:, along] for piece in pieces], axis=0), chunks(step), total, squares)
    products[...] = (total[...] * camera_scale[...]).T * inverse_rms(squares[...], features)


def last_kernel(
    pieces, earlier, sources, query_block, camera_block, counts, camera_scale, near, far, out, total, squares, placed
):
    features = near.shape[1]
    total[...] = jnp.zeros_like(total)
    squares[...] = jnp.zeros_like(squares)
    for step in range(features // CHUNK):
        along = pl.ds(step * CHUNK, CHUNK)
        panel = jnp.concatenate([piece[:, along] for piece in pieces], axis=0)
        add_products(panel, (near[:, along], far[:, along]), total, squares)
    products = (total[...] * camera_scale[...]).T * inverse_rms(squares[...], features)
    rows = pieces[0].shape[0]
    unit = 0
    for part in [*earlier, products]:
        for at in range(part.shape[0] // rows):
            start = pl.multiple_of(sources[unit] * rows, rows)
            placed[pl.ds(start, rows), :] = part[at * rows : (at + 1) * rows, :]
            unit += 1
    for slot in range(out.shape[0]):

        @pl.when(slot < counts[0, 0])
        def _():
            row = pl.multiple_of(query_block[0, 0, slot] * BLOCK, BLOCK)
            column = pl.multiple_of(camera_block[0, 0, slot] * BLOCK, BLOCK)
            out[slot] = placed[pl.ds(row, BLOCK), pl.ds(column, BLOCK)]

        @pl.when(slot >= counts[0, 0])
        def _():
            out[slot] = jnp.zeros((BLOCK, BLOCK), jnp.float32)


VMEM = pl.BlockSpec(memory_space=pltpu.VMEM)
SMEM = pl.BlockSpec(memory_space=pltpu.SMEM)
HBM = pl.BlockSpec(memory_space=pltpu.HBM)


def shards(queries, cameras, query_block, camera_block, counts):
    own = queries[0]
    mine = cameras[0]
    rows, features = own.shape
    tile = mine.shape[0]
    slots = query_block.shape[2]
    cores, core = lax.axis_size("blk"), lax.axis_index("blk")
    devices, me = lax.axis_size("query"), lax.axis_index("query")
    rings = devices // 4
    camera_rows = tile * cores
    pieces = {(0, 0): own}
    groups = []

    def tied(operand, *results):
        return lax.optimization_barrier((operand, *results))[0]

    def ring(flip, k, after=()):
        back = k > rings // 2
        pairs = [(i, (i + (-4 if back else 4)) % devices) for i in range(devices)]
        operand = pieces[flip, (k + 1) % rings if back else k - 1]
        pieces[flip, k] = lax.ppermute(tied(operand, *after), "query", pairs)

    def across(flip, bit, k, after=()):
        pairs = [(i, i ^ bit) for i in range(devices)]
        pieces[flip, k] = lax.ppermute(tied(pieces[flip ^ bit, k], *after), "query", pairs)

    def call(kernel, group, operands, specs, results, scratch, name):
        count = rows * len(group)
        groups.append(group)
        chosen = [pieces[unit] for unit in group if unit != (0, 0)]
        return pl.pallas_call(
            lambda *refs: kernel(refs[: len(chosen)], *refs[len(chosen) :]),
            in_specs=[VMEM] * len(chosen) + specs,
            out_specs=[VMEM] * len(results),
            out_shape=[jax.ShapeDtypeStruct(shape, dtype) for shape, dtype in results],
            scratch_shapes=[pltpu.VMEM((camera_rows, count), jnp.float32), pltpu.VMEM((count, 1), jnp.float32)] + scratch,
            compiler_params=pltpu.CompilerParams(vmem_limit_bytes=VMEM_LIMIT),
            cost_estimate=pl.CostEstimate(
                flops=2 * count * camera_rows * features,
                bytes_accessed=2 * features * (count + camera_rows),
                transcendentals=0,
            ),
            name=name,
        )(*chosen, *operands)

    def scaled(group):
        return ((rows * len(group), camera_rows), jnp.float32)

    outward = []
    for k in range(1, rings // 2 + 1):
        outward += [k] if k == rings - k else [k, rings - k]
    near_k, later = outward[0], outward[1:]

    ring(0, near_k)
    across(1, 1, 0)
    across(2, 2, 0)
    other = lax.ppermute(mine, "blk", [(i, (i + 1) % cores) for i in range(cores)])
    for k in later[:1]:
        ring(0, k, [other, pieces[1, 0], pieces[2, 0]])
    across(1, 1, near_k, [pieces[1, 0]])
    across(2, 2, near_k, [pieces[2, 0]])
    group = list(pieces)
    across(3, 2, 0, [pieces[1, near_k]])
    for k in later[1:2]:
        ring(0, k, [pieces[1, near_k]])
    across(3, 1, near_k)
    for k in later[:1]:
        across(2, 2, k, [pieces[2, near_k]])
    panels = [pltpu.with_memory_space_constraint(x, pltpu.HBM) for x in (own, mine, other)]
    first, camera_scale = call(
        early_kernel,
        group,
        panels,
        [HBM] * 3,
        [scaled(group), ((camera_rows, 1), jnp.float32)],
        [pltpu.VMEM(own.shape, own.dtype)]
        + [pltpu.VMEM((tile, AHEAD * CHUNK), mine.dtype)] * 2
        + [pltpu.SemaphoreType.DMA((3, features // CHUNK))],
        "early_products",
    )
    for at, k in enumerate(later):
        for further in later[at + 2 : at + 3]:
            ring(0, further, [pieces[1, later[at - 1]] if at else pieces[3, 0]])
        if at == 0:
            across(1, 1, k, [pieces[3, 0], first])
        elif at < len(later) - 1:
            across(2, 2, k, [pieces[2, later[at - 1]]])
            across(1, 1, k, [pieces[1, later[at - 1]]])
        else:
            across(1, 1, k)
            across(2, 2, k)
        ring(3, k, [pieces[2, later[at - 1]]] if at else [first])
    rest = [unit for unit in pieces if unit not in group]
    group = rest[:-LATE]
    second, near, far = call(
        middle_kernel,
        group,
        panels[1:] + [camera_scale],
        [HBM] * 2 + [VMEM],
        [scaled(group), (mine.shape, mine.dtype), (mine.shape, mine.dtype)],
        [pltpu.SemaphoreType.DMA((2, features // CHUNK))],
        "products",
    )
    earlier = [first, second]
    group = rest[-LATE:]

    block_places = tile // BLOCK
    owner = camera_block // block_places
    place = (core - owner) % cores * block_places + camera_block % block_places
    order = [unit for done in groups + [group] for unit in done]
    sources = jnp.stack([(me - 4 * k) % devices ^ flip for flip, k in order]).astype(jnp.int32)

    def closing(chosen, *refs):
        last_kernel(chosen, refs[: len(earlier)], *refs[len(earlier) :])

    (scores,) = call(
        closing,
        group,
        earlier + [sources, query_block, place, counts, camera_scale, near, far],
        [VMEM] * len(earlier) + [SMEM] * 4 + [VMEM] * 3,
        [((slots, BLOCK, BLOCK), jnp.float32)],
        [pltpu.VMEM((len(order) * rows, camera_rows), jnp.float32)],
        "scores",
    )
    return scores[None, None]


def solution(mesh):
    placed = (
        P("blk", ("parts", "query"), None),
        P(("parts", "query"), "blk", None),
        P(("parts", "query"), "blk", None),
        P(("parts", "query"), "blk", None),
        P(("parts", "query"), "blk"),
    )
    return jax.shard_map(
        shards,
        mesh=mesh,
        in_specs=placed,
        out_specs=P(("parts", "query"), "blk", None, None, None),
        check_vma=False,
    )
```

```python
import math

import jax
import jax.numpy as jnp
from jax import lax
from jax.experimental import pallas as pl
from jax.experimental.pallas import tpu as pltpu
from jax.sharding import PartitionSpec as P

BLOCK = 128
CHUNK = 4096
AHEAD = 2
VMEM_LIMIT = 20 * 1024 * 1024

ORDER = "c1 x0 y0 other c2 x1 y1 d0 c3 d1 y2 x2 d2 x3 y3 d3"
TIES = {
    "c2": "other x0 y0",
    "y1": "y0",
    "d0": "x1",
    "c3": "x1",
    "y2": "y1",
    "x2": "d0 early",
    "d2": "early",
    "d3": "y2",
}
EARLY = "c0 c1 x0 y0 c2 x1 y1"
LATE = "x3 y3 d3"


def add_products(panel, cameras, total, squares):
    at = 0
    for tile in cameras:
        total[at : at + tile.shape[0], :] += lax.dot_general(
            tile, panel, (((1,), (1,)), ((), ())), preferred_element_type=jnp.float32
        )
        at += tile.shape[0]
    wide = panel.astype(jnp.float32)
    squares[...] += jnp.sum(wide * wide, axis=-1, keepdims=True)


def inverse_rms(squares, features):
    return lax.rsqrt(squares * (1.0 / features) + 1e-06)


def chunks_of(sources, targets, sems):
    steps = sources[0].shape[1] // CHUNK
    steps_held = [target.shape[1] // CHUNK for target in targets]

    def at(step, count):
        return pl.ds(step % count * CHUNK, CHUNK)

    def copies(step):
        return [
            pltpu.make_async_copy(
                source.at[:, at(step, steps)], target.at[:, at(step, count)], sems.at[index, step % steps]
            )
            for index, (source, target, count) in enumerate(zip(sources, targets, steps_held))
        ]

    return steps, copies, lambda step: [target[:, at(step, count)] for target, count in zip(targets, steps_held)]


def early_kernel(pieces, own, mine, other, products, camera_scale, total, squares, held, near, far, sems):
    features = own.shape[1]
    steps, copies, chunks = chunks_of((mine, other, own), (near, far, held), sems)
    for step in range(min(AHEAD, steps)):
        for copy in copies(step):
            copy.start()
    total[...] = jnp.zeros_like(total)
    squares[...] = jnp.zeros_like(squares)
    camera_scale[...] = jnp.zeros_like(camera_scale)
    for step in range(steps):
        for copy in copies(step):
            copy.wait()
        *cameras, rows = chunks(step)
        along = pl.ds(step * CHUNK, CHUNK)
        add_products(jnp.concatenate([rows] + [piece[:, along] for piece in pieces], axis=0), cameras, total, squares)
        at = 0
        for tile in cameras:
            wide = tile.astype(jnp.float32)
            camera_scale[at : at + tile.shape[0], :] += jnp.sum(wide * wide, axis=-1, keepdims=True)
            at += tile.shape[0]
        if step + AHEAD < steps:
            for copy in copies(step + AHEAD):
                copy.start()
    camera_scale[...] = inverse_rms(camera_scale[...], features) * (1.0 / math.sqrt(features))
    products[...] = (total[...] * camera_scale[...]).T * inverse_rms(squares[...], features)


def middle_kernel(pieces, mine, other, camera_scale, products, near, far, total, squares, sems):
    features = near.shape[1]
    steps, copies, chunks = chunks_of((mine, other), (near, far), sems)
    for step in range(min(AHEAD, steps)):
        for copy in copies(step):
            copy.start()
    total[...] = jnp.zeros_like(total)
    squares[...] = jnp.zeros_like(squares)
    for step in range(steps):
        for copy in copies(step):
            copy.wait()
        if step + AHEAD < steps:
            for copy in copies(step + AHEAD):
                copy.start()
        along = pl.ds(step * CHUNK, CHUNK)
        add_products(jnp.concatenate([piece[:, along] for piece in pieces], axis=0), chunks(step), total, squares)
    products[...] = (total[...] * camera_scale[...]).T * inverse_rms(squares[...], features)


def last_kernel(
    pieces, earlier, sources, query_block, camera_block, counts, camera_scale, near, far, out, total, squares, placed
):
    features = near.shape[1]
    total[...] = jnp.zeros_like(total)
    squares[...] = jnp.zeros_like(squares)
    for step in range(features // CHUNK):
        along = pl.ds(step * CHUNK, CHUNK)
        panel = jnp.concatenate([piece[:, along] for piece in pieces], axis=0)
        add_products(panel, (near[:, along], far[:, along]), total, squares)
    products = (total[...] * camera_scale[...]).T * inverse_rms(squares[...], features)
    rows = pieces[0].shape[0]
    unit = 0
    for part in [*earlier, products]:
        for at in range(part.shape[0] // rows):
            start = pl.multiple_of(sources[unit] * rows, rows)
            placed[pl.ds(start, rows), :] = part[at * rows : (at + 1) * rows, :]
            unit += 1
    for slot in range(out.shape[0]):

        @pl.when(slot < counts[0, 0])
        def _():
            row = pl.multiple_of(query_block[0, 0, slot] * BLOCK, BLOCK)
            column = pl.multiple_of(camera_block[0, 0, slot] * BLOCK, BLOCK)
            out[slot] = placed[pl.ds(row, BLOCK), pl.ds(column, BLOCK)]

        @pl.when(slot >= counts[0, 0])
        def _():
            out[slot] = jnp.zeros((BLOCK, BLOCK), jnp.float32)


VMEM = pl.BlockSpec(memory_space=pltpu.VMEM)
SMEM = pl.BlockSpec(memory_space=pltpu.SMEM)
HBM = pl.BlockSpec(memory_space=pltpu.HBM)


def shards(queries, cameras, query_block, camera_block, counts):
    own = queries[0]
    mine = cameras[0]
    rows, features = own.shape
    tile = mine.shape[0]
    slots = query_block.shape[2]
    cores, core = lax.axis_size("blk"), lax.axis_index("blk")
    devices, me = lax.axis_size("query"), lax.axis_index("query")
    rings = devices // 4
    camera_rows = tile * cores
    pieces = {"c0": own}

    def behind(place):
        return (place + 1) // 2 if place % 2 else -(place // 2)

    def ring(name, place):
        by = 4 if place % 2 else -4
        pairs = [(i, (i + by) % devices) for i in range(devices)]
        return name + str(max(place - 2, 0 if name == "c" else place % 2)), pairs

    def swap(name, bit):
        return name, [(i, i ^ bit) for i in range(devices)]

    def permute(name):
        kind, place = name[0], int(name[1:])
        if kind == "c" or kind == "d" and place > 1:
            source, pairs = ring(kind, place)
        else:
            source, pairs = {
                "x": swap("c" + name[1:], 1),
                "y": swap("c" + name[1:], 2),
                "d": swap("y1", 1) if place else swap("x0", 2),
            }[kind]
        operand = lax.optimization_barrier((pieces[source], *[pieces[tie] for tie in TIES.get(name, "").split()]))[0]
        pieces[name] = lax.ppermute(operand, "query", pairs)

    def call(kernel, group, operands, specs, results, scratch, name):
        count = rows * len(group)
        chosen = [pieces[unit] for unit in group if unit != "c0"]
        return pl.pallas_call(
            lambda *refs: kernel(refs[: len(chosen)], *refs[len(chosen) :]),
            in_specs=[VMEM] * len(chosen) + specs,
            out_specs=[VMEM] * len(results),
            out_shape=[jax.ShapeDtypeStruct(shape, dtype) for shape, dtype in results],
            scratch_shapes=[pltpu.VMEM((camera_rows, count), jnp.float32), pltpu.VMEM((count, 1), jnp.float32)] + scratch,
            compiler_params=pltpu.CompilerParams(vmem_limit_bytes=VMEM_LIMIT),
            cost_estimate=pl.CostEstimate(
                flops=2 * count * camera_rows * features,
                bytes_accessed=2 * features * (count + camera_rows),
                transcendentals=0,
            ),
            name=name,
        )(*chosen, *operands)

    def scaled(group):
        return ((rows * len(group), camera_rows), jnp.float32)

    others = [kind + str(place) for place in range(4, rings) for kind in "cxyd"]
    groups = [EARLY.split(), [], LATE.split()]
    groups[1] = [name for name in ORDER.split() + others if name != "other" and name not in groups[0] + groups[2]]
    for name in ORDER.split() + others:
        if name == "other":
            pieces[name] = lax.ppermute(mine, "blk", [(i, (i + 1) % cores) for i in range(cores)])
            panels = [pltpu.with_memory_space_constraint(x, pltpu.HBM) for x in (own, mine, pieces[name])]
        else:
            permute(name)
        if "early" not in pieces and all(unit in pieces for unit in groups[0]):
            pieces["early"], camera_scale = call(
                early_kernel,
                groups[0],
                panels,
                [HBM] * 3,
                [scaled(groups[0]), ((camera_rows, 1), jnp.float32)],
                [pltpu.VMEM(own.shape, own.dtype)]
                + [pltpu.VMEM((tile, AHEAD * CHUNK), mine.dtype)] * 2
                + [pltpu.SemaphoreType.DMA((3, features // CHUNK))],
                "early_products",
            )
    second, near, far = call(
        middle_kernel,
        groups[1],
        panels[1:] + [camera_scale],
        [HBM] * 2 + [VMEM],
        [scaled(groups[1]), (mine.shape, mine.dtype), (mine.shape, mine.dtype)],
        [pltpu.SemaphoreType.DMA((2, features // CHUNK))],
        "products",
    )
    earlier = [pieces["early"], second]

    block_places = tile // BLOCK
    owner = camera_block // block_places
    place = (core - owner) % cores * block_places + camera_block % block_places
    order = [unit for group in groups for unit in group]
    sources = [(me - 4 * behind(int(unit[1:]))) % devices ^ "cxyd".index(unit[0]) for unit in order]
    sources = jnp.stack(sources).astype(jnp.int32)

    def closing(chosen, *refs):
        last_kernel(chosen, refs[: len(earlier)], *refs[len(earlier) :])

    (scores,) = call(
        closing,
        groups[2],
        earlier + [sources, query_block, place, counts, camera_scale, near, far],
        [VMEM] * len(earlier) + [SMEM] * 4 + [VMEM] * 3,
        [((slots, BLOCK, BLOCK), jnp.float32)],
        [pltpu.VMEM((len(order) * rows, camera_rows), jnp.float32)],
        "scores",
    )
    return scores[None, None]


def solution(mesh):
    placed = (
        P("blk", ("parts", "query"), None),
        P(("parts", "query"), "blk", None),
        P(("parts", "query"), "blk", None),
        P(("parts", "query"), "blk", None),
        P(("parts", "query"), "blk"),
    )
    return jax.shard_map(
        shards,
        mesh=mesh,
        in_specs=placed,
        out_specs=P(("parts", "query"), "blk", None, None, None),
        check_vma=False,
    )
```

```python
import math

import jax
import jax.numpy as jnp
from jax import lax
from jax.experimental import pallas as pl
from jax.experimental.pallas import tpu as pltpu
from jax.sharding import PartitionSpec as P

BLOCK = 128
CHUNK = 4096
AHEAD = 2
VMEM_LIMIT = 20 * 1024 * 1024

ORDER = ("c1", "x0", "y0", "other", "c2", "x1", "y1", "d0", "c3", "d1", "y2", "x2", "d2", "x3", "y3", "d3")
TIES = {
    "c2": ("other", "x0", "y0"),
    "y1": ("y0",),
    "d0": ("x1",),
    "c3": ("x1",),
    "y2": ("y1",),
    "x2": ("d0", "early"),
    "d2": ("early",),
    "d3": ("y2",),
}
EARLY = ("c0", "c1", "x0", "y0", "c2", "x1", "y1")
LATE = ("x3", "y3", "d3")


def add_products(panel, cameras, total, squares):
    at = 0
    for tile in cameras:
        total[at : at + tile.shape[0], :] += lax.dot_general(
            tile, panel, (((1,), (1,)), ((), ())), preferred_element_type=jnp.float32
        )
        at += tile.shape[0]
    wide = panel.astype(jnp.float32)
    squares[...] += jnp.sum(wide * wide, axis=-1, keepdims=True)


def inverse_rms(squares, features):
    return lax.rsqrt(squares * (1.0 / features) + 1e-06)


def chunks_of(sources, targets, sems):
    steps = sources[0].shape[1] // CHUNK
    steps_held = [target.shape[1] // CHUNK for target in targets]

    def at(step, count):
        return pl.ds(step % count * CHUNK, CHUNK)

    def copies(step):
        return [
            pltpu.make_async_copy(
                source.at[:, at(step, steps)], target.at[:, at(step, count)], sems.at[index, step % steps]
            )
            for index, (source, target, count) in enumerate(zip(sources, targets, steps_held))
        ]

    return steps, copies, lambda step: [target[:, at(step, count)] for target, count in zip(targets, steps_held)]


def early_kernel(pieces, own, mine, other, products, camera_scale, total, squares, held, near, far, sems):
    features = own.shape[1]
    steps, copies, chunks = chunks_of((mine, other, own), (near, far, held), sems)
    for step in range(min(AHEAD, steps)):
        for copy in copies(step):
            copy.start()
    total[...] = jnp.zeros_like(total)
    squares[...] = jnp.zeros_like(squares)
    camera_scale[...] = jnp.zeros_like(camera_scale)
    for step in range(steps):
        for copy in copies(step):
            copy.wait()
        *cameras, rows = chunks(step)
        along = pl.ds(step * CHUNK, CHUNK)
        add_products(jnp.concatenate([rows] + [piece[:, along] for piece in pieces], axis=0), cameras, total, squares)
        at = 0
        for tile in cameras:
            wide = tile.astype(jnp.float32)
            camera_scale[at : at + tile.shape[0], :] += jnp.sum(wide * wide, axis=-1, keepdims=True)
            at += tile.shape[0]
        if step + AHEAD < steps:
            for copy in copies(step + AHEAD):
                copy.start()
    camera_scale[...] = inverse_rms(camera_scale[...], features) * (1.0 / math.sqrt(features))
    products[...] = (total[...] * camera_scale[...]).T * inverse_rms(squares[...], features)


def middle_kernel(pieces, mine, other, camera_scale, products, near, far, total, squares, sems):
    features = near.shape[1]
    steps, copies, chunks = chunks_of((mine, other), (near, far), sems)
    for step in range(min(AHEAD, steps)):
        for copy in copies(step):
            copy.start()
    total[...] = jnp.zeros_like(total)
    squares[...] = jnp.zeros_like(squares)
    for step in range(steps):
        for copy in copies(step):
            copy.wait()
        if step + AHEAD < steps:
            for copy in copies(step + AHEAD):
                copy.start()
        along = pl.ds(step * CHUNK, CHUNK)
        add_products(jnp.concatenate([piece[:, along] for piece in pieces], axis=0), chunks(step), total, squares)
    products[...] = (total[...] * camera_scale[...]).T * inverse_rms(squares[...], features)


def last_kernel(
    pieces, earlier, sources, query_block, camera_block, counts, camera_scale, near, far, out, total, squares, placed
):
    features = near.shape[1]
    total[...] = jnp.zeros_like(total)
    squares[...] = jnp.zeros_like(squares)
    half = features // 2
    for part in range(2):
        along = pl.ds(part * half, half)
        panel = jnp.concatenate([piece[:, along] for piece in pieces], axis=0)
        add_products(panel, (near[:, along], far[:, along]), total, squares)
    products = (total[...] * camera_scale[...]).T * inverse_rms(squares[...], features)
    rows = pieces[0].shape[0]
    unit = 0
    for part in [*earlier, products]:
        for at in range(part.shape[0] // rows):
            start = pl.multiple_of(sources[unit] * rows, rows)
            placed[pl.ds(start, rows), :] = part[at * rows : (at + 1) * rows, :]
            unit += 1
    for slot in range(out.shape[0]):

        @pl.when(slot < counts[0, 0])
        def _():
            row = pl.multiple_of(query_block[0, 0, slot] * BLOCK, BLOCK)
            column = pl.multiple_of(camera_block[0, 0, slot] * BLOCK, BLOCK)
            out[slot] = placed[pl.ds(row, BLOCK), pl.ds(column, BLOCK)]

        @pl.when(slot >= counts[0, 0])
        def _():
            out[slot] = jnp.zeros((BLOCK, BLOCK), jnp.float32)


VMEM = pl.BlockSpec(memory_space=pltpu.VMEM)
SMEM = pl.BlockSpec(memory_space=pltpu.SMEM)
HBM = pl.BlockSpec(memory_space=pltpu.HBM)


def shards(queries, cameras, query_block, camera_block, counts):
    own = queries[0]
    mine = cameras[0]
    rows, features = own.shape
    tile = mine.shape[0]
    slots = query_block.shape[2]
    cores, core = lax.axis_size("blk"), lax.axis_index("blk")
    devices, me = lax.axis_size("query"), lax.axis_index("query")
    rings = devices // 4
    camera_rows = tile * cores
    pieces = {"c0": own}

    def behind(place):
        return (place + 1) // 2 if place % 2 else -(place // 2)

    def ring(name, place):
        by = 4 if place % 2 else -4
        pairs = [(i, (i + by) % devices) for i in range(devices)]
        return name + str(max(place - 2, 0 if name == "c" else place % 2)), pairs

    def swap(name, bit):
        return name, [(i, i ^ bit) for i in range(devices)]

    def permute(name):
        kind, place = name[0], int(name[1:])
        if kind == "c" or kind == "d" and place > 1:
            source, pairs = ring(kind, place)
        else:
            source, pairs = {
                "x": swap("c" + name[1:], 1),
                "y": swap("c" + name[1:], 2),
                "d": swap("y1", 1) if place else swap("x0", 2),
            }[kind]
        operand = lax.optimization_barrier((pieces[source], *[pieces[tie] for tie in TIES.get(name, ())]))[0]
        pieces[name] = lax.ppermute(operand, "query", pairs)

    def call(kernel, group, operands, specs, results, scratch, name):
        count = rows * len(group)
        chosen = [pieces[unit] for unit in group if unit != "c0"]
        return pl.pallas_call(
            lambda *refs: kernel(refs[: len(chosen)], *refs[len(chosen) :]),
            in_specs=[VMEM] * len(chosen) + specs,
            out_specs=[VMEM] * len(results),
            out_shape=[jax.ShapeDtypeStruct(shape, dtype) for shape, dtype in results],
            scratch_shapes=[pltpu.VMEM((camera_rows, count), jnp.float32), pltpu.VMEM((count, 1), jnp.float32)] + scratch,
            compiler_params=pltpu.CompilerParams(vmem_limit_bytes=VMEM_LIMIT),
            cost_estimate=pl.CostEstimate(
                flops=2 * count * camera_rows * features,
                bytes_accessed=2 * features * (count + camera_rows),
                transcendentals=0,
            ),
            name=name,
        )(*chosen, *operands)

    def scaled(group):
        return ((rows * len(group), camera_rows), jnp.float32)

    others = [kind + str(place) for place in range(4, rings) for kind in "cxyd"]
    groups = [EARLY, [], LATE]
    groups[1] = [name for name in [*ORDER, *others] if name != "other" and name not in EARLY + LATE]
    for name in [*ORDER, *others]:
        if name == "other":
            pieces[name] = lax.ppermute(mine, "blk", [(i, (i + 1) % cores) for i in range(cores)])
            panels = [pltpu.with_memory_space_constraint(x, pltpu.HBM) for x in (own, mine, pieces[name])]
        else:
            permute(name)
        if "early" not in pieces and all(unit in pieces for unit in groups[0]):
            pieces["early"], camera_scale = call(
                early_kernel,
                groups[0],
                panels,
                [HBM] * 3,
                [scaled(groups[0]), ((camera_rows, 1), jnp.float32)],
                [pltpu.VMEM(own.shape, own.dtype)]
                + [pltpu.VMEM((tile, AHEAD * CHUNK), mine.dtype)] * 2
                + [pltpu.SemaphoreType.DMA((3, features // CHUNK))],
                "early_products",
            )
    second, near, far = call(
        middle_kernel,
        groups[1],
        panels[1:] + [camera_scale],
        [HBM] * 2 + [VMEM],
        [scaled(groups[1]), (mine.shape, mine.dtype), (mine.shape, mine.dtype)],
        [pltpu.SemaphoreType.DMA((2, features // CHUNK))],
        "products",
    )
    earlier = [pieces["early"], second]

    block_places = tile // BLOCK
    owner = camera_block // block_places
    place = (core - owner) % cores * block_places + camera_block % block_places
    order = [unit for group in groups for unit in group]
    sources = [(me - 4 * behind(int(unit[1:]))) % devices ^ "cxyd".index(unit[0]) for unit in order]
    sources = jnp.stack(sources).astype(jnp.int32)

    def closing(chosen, *refs):
        last_kernel(chosen, refs[: len(earlier)], *refs[len(earlier) :])

    (scores,) = call(
        closing,
        groups[2],
        earlier + [sources, query_block, place, counts, camera_scale, near, far],
        [VMEM] * len(earlier) + [SMEM] * 4 + [VMEM] * 3,
        [((slots, BLOCK, BLOCK), jnp.float32)],
        [pltpu.VMEM((len(order) * rows, camera_rows), jnp.float32)],
        "scores",
    )
    return scores[None, None]


def solution(mesh):
    placed = (
        P("blk", ("parts", "query"), None),
        P(("parts", "query"), "blk", None),
        P(("parts", "query"), "blk", None),
        P(("parts", "query"), "blk", None),
        P(("parts", "query"), "blk"),
    )
    return jax.shard_map(
        shards,
        mesh=mesh,
        in_specs=placed,
        out_specs=P(("parts", "query"), "blk", None, None, None),
        check_vma=False,
    )
```

```python
import math

import jax
import jax.numpy as jnp
from jax import lax
from jax.experimental import pallas as pl
from jax.experimental.pallas import tpu as pltpu
from jax.sharding import PartitionSpec as P

BLOCK = 128
CHUNK = 4096
AHEAD = 2
VMEM_LIMIT = 20 * 1024 * 1024

ORDER = ("c1", "x0", "y0", "other", "c2", "x1", "y1", "d0", "c3", "d1", "y2", "x2", "d2", "x3", "y3", "d3")
TIES = {
    "c2": ("other", "x0"),
    "y1": ("y0",),
    "d0": ("x1",),
    "c3": ("x1",),
    "y2": ("y1",),
    "x2": ("d0", "early"),
    "d2": ("early",),
    "d3": ("y2",),
}
EARLY = ("c0", "c1", "x0", "y0", "c2", "x1", "y1")
LATE = ("x3", "y3", "d3")


def add_products(panel, cameras, total, squares):
    at = 0
    for tile in cameras:
        total[at : at + tile.shape[0], :] += lax.dot_general(
            tile, panel, (((1,), (1,)), ((), ())), preferred_element_type=jnp.float32
        )
        at += tile.shape[0]
    wide = panel.astype(jnp.float32)
    squares[...] += jnp.sum(wide * wide, axis=-1, keepdims=True)


def inverse_rms(squares, features):
    return lax.rsqrt(squares * (1.0 / features) + 1e-06)


def chunks_of(sources, targets, sems):
    steps = sources[0].shape[1] // CHUNK
    steps_held = [target.shape[1] // CHUNK for target in targets]

    def at(step, count):
        return pl.ds(step % count * CHUNK, CHUNK)

    def copies(step):
        return [
            pltpu.make_async_copy(
                source.at[:, at(step, steps)], target.at[:, at(step, count)], sems.at[index, step % steps]
            )
            for index, (source, target, count) in enumerate(zip(sources, targets, steps_held))
        ]

    return steps, copies, lambda step: [target[:, at(step, count)] for target, count in zip(targets, steps_held)]


def early_kernel(pieces, own, mine, other, products, camera_scale, total, squares, held, near, far, sems):
    features = own.shape[1]
    steps, copies, chunks = chunks_of((mine, other, own), (near, far, held), sems)
    for step in range(min(AHEAD, steps)):
        for copy in copies(step):
            copy.start()
    total[...] = jnp.zeros_like(total)
    squares[...] = jnp.zeros_like(squares)
    camera_scale[...] = jnp.zeros_like(camera_scale)
    for step in range(steps):
        for copy in copies(step):
            copy.wait()
        *cameras, rows = chunks(step)
        along = pl.ds(step * CHUNK, CHUNK)
        add_products(jnp.concatenate([rows] + [piece[:, along] for piece in pieces], axis=0), cameras, total, squares)
        at = 0
        for tile in cameras:
            wide = tile.astype(jnp.float32)
            camera_scale[at : at + tile.shape[0], :] += jnp.sum(wide * wide, axis=-1, keepdims=True)
            at += tile.shape[0]
        if step + AHEAD < steps:
            for copy in copies(step + AHEAD):
                copy.start()
    camera_scale[...] = inverse_rms(camera_scale[...], features) * (1.0 / math.sqrt(features))
    products[...] = (total[...] * camera_scale[...]).T * inverse_rms(squares[...], features)


def middle_kernel(pieces, mine, other, camera_scale, products, near, far, total, squares, sems):
    features = near.shape[1]
    steps, copies, chunks = chunks_of((mine, other), (near, far), sems)
    for step in range(min(AHEAD, steps)):
        for copy in copies(step):
            copy.start()
    total[...] = jnp.zeros_like(total)
    squares[...] = jnp.zeros_like(squares)
    for step in range(steps):
        for copy in copies(step):
            copy.wait()
        if step + AHEAD < steps:
            for copy in copies(step + AHEAD):
                copy.start()
        along = pl.ds(step * CHUNK, CHUNK)
        add_products(jnp.concatenate([piece[:, along] for piece in pieces], axis=0), chunks(step), total, squares)
    products[...] = (total[...] * camera_scale[...]).T * inverse_rms(squares[...], features)


def last_kernel(
    pieces, earlier, sources, query_block, camera_block, counts, camera_scale, near, far, out, total, squares, placed
):
    features = near.shape[1]
    total[...] = jnp.zeros_like(total)
    squares[...] = jnp.zeros_like(squares)
    half = features // 2
    for part in range(2):
        along = pl.ds(part * half, half)
        panel = jnp.concatenate([piece[:, along] for piece in pieces], axis=0)
        add_products(panel, (near[:, along], far[:, along]), total, squares)
    products = (total[...] * camera_scale[...]).T * inverse_rms(squares[...], features)
    rows = pieces[0].shape[0]
    unit = 0
    for part in [*earlier, products]:
        for at in range(part.shape[0] // rows):
            start = pl.multiple_of(sources[unit] * rows, rows)
            placed[pl.ds(start, rows), :] = part[at * rows : (at + 1) * rows, :]
            unit += 1
    for slot in range(out.shape[0]):

        @pl.when(slot < counts[0, 0])
        def _():
            row = pl.multiple_of(query_block[0, 0, slot] * BLOCK, BLOCK)
            column = pl.multiple_of(camera_block[0, 0, slot] * BLOCK, BLOCK)
            out[slot] = placed[pl.ds(row, BLOCK), pl.ds(column, BLOCK)]

        @pl.when(slot >= counts[0, 0])
        def _():
            out[slot] = jnp.zeros((BLOCK, BLOCK), jnp.float32)


VMEM = pl.BlockSpec(memory_space=pltpu.VMEM)
SMEM = pl.BlockSpec(memory_space=pltpu.SMEM)
HBM = pl.BlockSpec(memory_space=pltpu.HBM)


def shards(queries, cameras, query_block, camera_block, counts):
    own = queries[0]
    mine = cameras[0]
    rows, features = own.shape
    tile = mine.shape[0]
    slots = query_block.shape[2]
    cores, core = lax.axis_size("blk"), lax.axis_index("blk")
    devices, me = lax.axis_size("query"), lax.axis_index("query")
    rings = devices // 4
    camera_rows = tile * cores
    pieces = {"c0": own}

    def behind(place):
        return (place + 1) // 2 if place % 2 else -(place // 2)

    def ring(name, place):
        by = 4 if place % 2 else -4
        pairs = [(i, (i + by) % devices) for i in range(devices)]
        return name + str(max(place - 2, 0 if name == "c" else place % 2)), pairs

    def swap(name, bit):
        return name, [(i, i ^ bit) for i in range(devices)]

    def permute(name):
        kind, place = name[0], int(name[1:])
        if kind == "c" or kind == "d" and place > 1:
            source, pairs = ring(kind, place)
        else:
            source, pairs = {
                "x": swap("c" + name[1:], 1),
                "y": swap("c" + name[1:], 2),
                "d": swap("y1", 1) if place else swap("x0", 2),
            }[kind]
        operand = lax.optimization_barrier((pieces[source], *[pieces[tie] for tie in TIES.get(name, ())]))[0]
        pieces[name] = lax.ppermute(operand, "query", pairs)

    def call(kernel, group, operands, specs, results, scratch, name):
        count = rows * len(group)
        chosen = [pieces[unit] for unit in group if unit != "c0"]
        return pl.pallas_call(
            lambda *refs: kernel(refs[: len(chosen)], *refs[len(chosen) :]),
            in_specs=[VMEM] * len(chosen) + specs,
            out_specs=[VMEM] * len(results),
            out_shape=[jax.ShapeDtypeStruct(shape, dtype) for shape, dtype in results],
            scratch_shapes=[pltpu.VMEM((camera_rows, count), jnp.float32), pltpu.VMEM((count, 1), jnp.float32)] + scratch,
            compiler_params=pltpu.CompilerParams(vmem_limit_bytes=VMEM_LIMIT),
            cost_estimate=pl.CostEstimate(
                flops=2 * count * camera_rows * features,
                bytes_accessed=2 * features * (count + camera_rows),
                transcendentals=0,
            ),
            name=name,
        )(*chosen, *operands)

    def scaled(group):
        return ((rows * len(group), camera_rows), jnp.float32)

    others = [kind + str(place) for place in range(4, rings) for kind in "cxyd"]
    groups = [EARLY, [], LATE]
    groups[1] = [name for name in [*ORDER, *others] if name != "other" and name not in EARLY + LATE]
    for name in [*ORDER, *others]:
        if name == "other":
            pieces[name] = lax.ppermute(mine, "blk", [(i, (i + 1) % cores) for i in range(cores)])
            panels = [pltpu.with_memory_space_constraint(x, pltpu.HBM) for x in (own, mine, pieces[name])]
        else:
            permute(name)
        if "early" not in pieces and all(unit in pieces for unit in groups[0]):
            pieces["early"], camera_scale = call(
                early_kernel,
                groups[0],
                panels,
                [HBM] * 3,
                [scaled(groups[0]), ((camera_rows, 1), jnp.float32)],
                [pltpu.VMEM(own.shape, own.dtype)]
                + [pltpu.VMEM((tile, AHEAD * CHUNK), mine.dtype)] * 2
                + [pltpu.SemaphoreType.DMA((3, features // CHUNK))],
                "early_products",
            )
    second, near, far = call(
        middle_kernel,
        groups[1],
        panels[1:] + [camera_scale],
        [HBM] * 2 + [VMEM],
        [scaled(groups[1]), (mine.shape, mine.dtype), (mine.shape, mine.dtype)],
        [pltpu.SemaphoreType.DMA((2, features // CHUNK))],
        "products",
    )
    earlier = [pieces["early"], second]

    block_places = tile // BLOCK
    owner = camera_block // block_places
    place = (core - owner) % cores * block_places + camera_block % block_places
    order = [unit for group in groups for unit in group]
    sources = [(me - 4 * behind(int(unit[1:]))) % devices ^ "cxyd".index(unit[0]) for unit in order]
    sources = jnp.stack(sources).astype(jnp.int32)

    def closing(chosen, *refs):
        last_kernel(chosen, refs[: len(earlier)], *refs[len(earlier) :])

    (scores,) = call(
        closing,
        groups[2],
        earlier + [sources, query_block, place, counts, camera_scale, near, far],
        [VMEM] * len(earlier) + [SMEM] * 4 + [VMEM] * 3,
        [((slots, BLOCK, BLOCK), jnp.float32)],
        [pltpu.VMEM((len(order) * rows, camera_rows), jnp.float32)],
        "scores",
    )
    return scores[None, None]


def solution(mesh):
    placed = (
        P("blk", ("parts", "query"), None),
        P(("parts", "query"), "blk", None),
        P(("parts", "query"), "blk", None),
        P(("parts", "query"), "blk", None),
        P(("parts", "query"), "blk"),
    )
    return jax.shard_map(
        shards,
        mesh=mesh,
        in_specs=placed,
        out_specs=P(("parts", "query"), "blk", None, None, None),
        check_vma=False,
    )
```
